128 devices in a mesh: row: 16 (over y_lo, x, core), col: 8 (over z, y_hi).
Axes of the slice: x: 4, y: 4 (y_hi: 2, y_lo: 2; y = y_hi * 2 + y_lo), z: 4, core: 2. Of those that a mesh axis runs over, the one named last changes fastest.
Arguments:
- velocity: float32 [2, 4096, 4096], P(None, 'row', 'col'), may hold values from -6 to 6
Outputs:
- restart: float32 [2, 8192, 8192], P(None, ('row', 'col'))
The draws below stay inside these ranges and needn't reach their ends.
All inputs are finite; a program needn't handle non-finite values.
Results may differ from the reference program's by a relative error of at most 0.00007.
Values sent between devices are 32-bit elements; how exact they have to be, the bound alone decides.
A program may use at most 128 MiB of HBM per device.

```python
import jax
import jax.numpy as jnp
from jax import lax

OLD_N = 4096
PLANES = 2
NEW_N = 8192


def steps_of(rng, extent, cuts, smallest, top_value):
    level = 1.0
    for dim, shards_of in cuts:
        draws = jax.random.uniform(jax.random.fold_in(jax.random.fold_in(rng, 6), dim), (shards_of,), jnp.float32, smallest / len(cuts), top_value / len(cuts))
        level = level * jnp.repeat(jnp.exp(draws), extent[dim] // shards_of).reshape((-1,) + (1,) * (len(extent) - 1 - dim))
    return level


def noise(rng, shape, deviation, limit, split=(), kind=jnp.bfloat16):
    drawn = jax.random.normal(rng, shape, jnp.float32) * deviation
    if len(split) > 0:
        drawn = steps_of(rng, shape, split, -0.22, 0.18) * drawn
    return jnp.clip(drawn, min=-limit, max=limit).astype(kind)


def setup_inputs(seed: int = 0) -> dict:
    splits = jax.random.split(jax.random.key(seed), 2)
    velocity = noise(splits[0], (PLANES, OLD_N, OLD_N), 1.0, 6.0, ((1, 16), (2, 8)), jnp.float32)
    return dict(velocity=velocity)


def reference(velocity):
    def one_plane(plane):
        half_modes = OLD_N // 2
        spectrum = jnp.fft.rfft(plane, axis=1)[:, :half_modes]
        spectrum = jnp.fft.fft(spectrum, axis=0) / (OLD_N * OLD_N)
        spectrum = spectrum.at[half_modes].set(0.0)
        padded = jnp.zeros((NEW_N, half_modes), spectrum.dtype)
        padded = padded.at[:half_modes].set(spectrum[:half_modes])
        padded = padded.at[NEW_N - half_modes:].set(spectrum[half_modes:])
        lines = jnp.fft.ifft(padded, axis=0, norm="forward")
        full_half = jnp.zeros((NEW_N, NEW_N // 2 + 1), lines.dtype)
        full_half = full_half.at[:, :half_modes].set(lines)
        return jnp.fft.irfft(full_half, n=NEW_N, axis=1, norm="forward").astype(jnp.float32)

    return lax.map(one_plane, velocity)
```

```python
import functools

import jax
import jax.numpy as jnp
import ml_dtypes
import numpy as np
from jax import lax
from jax.experimental import pallas as pl
from jax.experimental.pallas import tpu as pltpu
from jax.sharding import PartitionSpec as P

OLD_N = 4096
RADIX = 16
BLOCK = 256
ROWS, COLS = 16, 8
MESH = pl.DeviceIdType.MESH
F32, BF16 = jnp.float32, jnp.bfloat16


def split_bf16(table):
    hi = table.astype(ml_dtypes.bfloat16)
    lo = (table - hi.astype(np.float64)).astype(ml_dtypes.bfloat16)
    return hi, lo


def phases(points, sign):
    angle = sign * 2.0 * np.pi * (np.arange(RADIX) - RADIX // 2)[:, None] * points[None, :] / OLD_N
    return np.stack([np.cos(angle), np.sin(angle)]).astype(np.float32)


def shift_kernel(points):
    s = points[None, :] - np.arange(BLOCK)[:, None]
    whole = s == np.round(s)
    safe = np.where(whole, 0.5, s)
    value = np.where(whole, (s == 0) * 1.0, np.sin(np.pi * safe) / (BLOCK * np.sin(np.pi * safe / BLOCK)))
    return value / RADIX


def dft4(parts, sign):
    (ar, ai), (br, bi), (cr, ci), (dr, di) = parts
    sr, si, er, ei = ar + cr, ai + ci, ar - cr, ai - ci
    tr, ti, fr, fi = br + dr, bi + di, br - dr, bi - di
    if sign < 0:
        fr, fi = -fr, -fi
    return [(sr + tr, si + ti), (er - fi, ei + fr), (sr - tr, si - ti), (er + fi, ei - fr)]


def dft16(parts, sign):
    half = [dft4([parts[4 * hi + lo] for hi in range(4)], sign) for lo in range(4)]
    out = [None] * 16
    for klo in range(4):
        column = []
        for lo in range(4):
            re, im = half[lo][klo]
            turn = lo * klo
            if turn == 4:
                re, im = (-im, re) if sign > 0 else (im, -re)
            elif turn:
                c = float(np.cos(2 * np.pi * turn / 16))
                s = float(sign * np.sin(2 * np.pi * turn / 16))
                if turn == 2:
                    re, im = (re - im) * c if sign > 0 else (re + im) * c, (im + re) * c if sign > 0 else (im - re) * c
                elif turn == 6:
                    re, im = (re * c - im * s, re * s + im * c)
                else:
                    re, im = (re * c - im * s, re * s + im * c)
            column.append((re, im))
        for khi, value in enumerate(dft4(column, sign)):
            out[klo + 4 * khi] = value
    return out


def drop_half_mode(re, im, alternate):
    tr = jnp.sum(re * alternate, axis=-1, keepdims=True) * (1.0 / BLOCK)
    ti = jnp.sum(im * alternate, axis=-1, keepdims=True) * (1.0 / BLOCK)
    return re - alternate * tr, im - alternate * ti


def turn_by(re, im, table, k, lanes):
    c, s = table[0, k : k + 1, lanes], table[1, k : k + 1, lanes]
    return re * c - im * s, re * s + im * c


def product(x, high, low):
    hi = x.astype(BF16)
    lo = (x - hi.astype(F32)).astype(BF16)
    dot = functools.partial(jnp.dot, preferred_element_type=F32)
    return dot(hi, high) + (dot(lo, high) + dot(hi, low))


def exchange_kernel(
    v_ref, pre_ref, post_ref, high_ref, low_ref, even_ref, odd_ref,
    turned, lines, spec, shifted, back, outbox, fixed, sums, all_sums, send_sem, recv_sem, token,
):
    r, c = lax.axis_index("row"), lax.axis_index("col")

    def row_peer(i):
        return lax.rem(r + i, ROWS)

    def col_peer(i):
        return lax.rem(c + i, COLS)

    barrier = pltpu.get_barrier_semaphore()

    @pl.loop(1, ROWS)
    def _(i):
        pl.semaphore_signal(barrier, inc=1, device_id={"row": row_peer(i), "col": c}, device_id_type=MESH)

    @pl.loop(1, COLS)
    def _(i):
        pl.semaphore_signal(barrier, inc=1, device_id={"row": r, "col": col_peer(i)}, device_id_type=MESH)

    @pl.loop(0, 8)
    def _(q):
        plane, tile = q // 4, q % 4
        lanes = pl.ds(pl.multiple_of(tile * 128, 128), 128)
        for half in range(2):
            block = v_ref[plane, half * 128 : half * 128 + 128, lanes].T
            turned[2 * q, :, half * 128 : half * 128 + 128] = block[:64]
            turned[2 * q + 1, :, half * 128 : half * 128 + 128] = block[64:]

    sign8 = 1.0 - 2.0 * (lax.broadcasted_iota(jnp.int32, (8, 512), 0) % 2).astype(F32)
    for plane in range(2):
        total = jnp.zeros((8, 512), F32)
        for g in range(32):
            total = total + v_ref[plane, 8 * g : 8 * g + 8, :]
        total = jnp.sum(total * sign8, axis=0, keepdims=True)
        for tile in range(4):
            sums[plane * 4 + tile : plane * 4 + tile + 1, :] = total[:, tile * 128 : tile * 128 + 128]

    lines[r] = turned[r]
    all_sums[r] = sums[...]

    pl.semaphore_wait(barrier, ROWS + COLS - 2)

    @pl.loop(1, COLS)
    def _(i):
        pl.semaphore_signal(token, inc=1, device_id={"row": r, "col": col_peer(i)}, device_id_type=MESH)

    @pl.loop(1, ROWS)
    def _(i):
        pltpu.make_async_remote_copy(
            sums, all_sums.at[r], send_sem.at[1], recv_sem.at[1],
            device_id={"row": row_peer(i), "col": c}, device_id_type=MESH,
        ).start()

    @pl.loop(1, ROWS)
    def _(i):
        pltpu.make_async_remote_copy(
            turned.at[row_peer(i)], lines.at[r], send_sem.at[0], recv_sem.at[0],
            device_id={"row": row_peer(i), "col": c}, device_id_type=MESH,
        ).start()

    others = all_sums.at[pl.ds(0, ROWS - 1)]
    pltpu.make_async_copy(others, others, recv_sem.at[1]).wait()
    nyquist = all_sums[0]
    for i in range(1, ROWS):
        nyquist = nyquist + all_sums[i]
    nyquist = nyquist * (1.0 / OLD_N)
    for plane in range(2):
        row = jnp.concatenate([nyquist[plane * 4 + tile : plane * 4 + tile + 1] for tile in range(4)], axis=1)
        correction = row * sign8
        for g in range(32):
            fixed[plane, 8 * g : 8 * g + 8, :] = v_ref[plane, 8 * g : 8 * g + 8, :] - correction

    def old_rows(peer):
        return fixed.at[:, pl.ds(pl.multiple_of(peer * 32, 32), 32), :]

    my_columns = even_ref.at[:, :, pl.ds(pl.multiple_of(c * 512, 512), 512)]

    @pl.loop(1, COLS)
    def _(i):
        pltpu.make_async_remote_copy(
            old_rows(col_peer(i)), my_columns, send_sem.at[2], recv_sem.at[2],
            device_id={"row": r, "col": col_peer(i)}, device_id_type=MESH,
        ).start()

    own_even = pltpu.make_async_copy(old_rows(c), my_columns, send_sem.at[4])
    own_even.start()

    others = lines.at[pl.ds(0, ROWS - 1)]
    pltpu.make_async_copy(others, others, recv_sem.at[0]).wait()

    alternate = 1.0 - 2.0 * (lax.broadcasted_iota(jnp.int32, (8, BLOCK), 1) % 2).astype(F32)

    @pl.loop(0, 4)
    def _(g):
        re_rows = pl.ds(pl.multiple_of(g * 8, 8), 8)
        im_rows = pl.ds(pl.multiple_of(g * 8 + 32, 8), 8)
        modes = dft16([(lines[b, re_rows, :], lines[b, im_rows, :]) for b in range(RADIX)], -1)
        modes[0] = drop_half_mode(*modes[0], alternate)
        for k in range(RADIX):
            re, im = turn_by(*modes[k], pre_ref, k, slice(None))
            spec[k, re_rows, :] = re
            spec[k, im_rows, :] = im

    @pl.loop(0, 4)
    def _(g):
        x = spec[pl.ds(g * 4, 4)].reshape(256, BLOCK)
        shifted[pl.ds(g * 4, 4)] = product(x, high_ref[...], low_ref[...]).reshape(4, 64, BLOCK)

    @pl.loop(0, 4)
    def _(g):
        re_rows = pl.ds(pl.multiple_of(g * 8, 8), 8)
        im_rows = pl.ds(pl.multiple_of(g * 8 + 32, 8), 8)
        for t in range(2):
            lanes = slice(t * 128, t * 128 + 128)
            modes = [
                turn_by(shifted[k, re_rows, lanes], shifted[k, im_rows, lanes], post_ref, k, lanes)
                for k in range(RADIX)
            ]
            points = dft16(modes, 1)
            for a in range(RADIX):
                back[a, t, re_rows, :] = points[a][0]
                back[a, t, im_rows, :] = points[a][1]

    pl.semaphore_wait(token, COLS - 1)

    @pl.loop(0, ROWS)
    def _(i):
        a = row_peer(i)
        outbox[a] = back[a].reshape(128, 128).T

        @pl.loop(0, COLS)
        def _(j):
            peer = col_peer(j)

            @pl.when(i + j > 0)
            def _():
                pltpu.make_async_remote_copy(
                    outbox.at[a, pl.ds(pl.multiple_of(peer * 16, 16), 16), :], odd_ref.at[r * COLS + c],
                    send_sem.at[3], recv_sem.at[3],
                    device_id={"row": a, "col": peer}, device_id_type=MESH,
                ).start()

    own_odd = pltpu.make_async_copy(
        outbox.at[r, pl.ds(pl.multiple_of(c * 16, 16), 16), :], odd_ref.at[r * COLS + c], send_sem.at[5]
    )
    own_odd.start()

    own_even.wait()
    own_odd.wait()
    sent = turned.at[pl.ds(0, ROWS - 1)]
    pltpu.make_async_copy(sent, sent, send_sem.at[0]).wait()
    sent = all_sums.at[pl.ds(0, ROWS - 1)]
    pltpu.make_async_copy(sent, sent, send_sem.at[1]).wait()
    sent = even_ref.at[:, :, pl.ds(0, 512 * (COLS - 1))]
    pltpu.make_async_copy(sent, sent, send_sem.at[2]).wait()
    pltpu.make_async_copy(sent, sent, recv_sem.at[2]).wait()
    sent = odd_ref.at[pl.ds(0, ROWS * COLS - 1)]
    pltpu.make_async_copy(sent, sent, send_sem.at[3]).wait()
    pltpu.make_async_copy(sent, sent, recv_sem.at[3]).wait()


def refine_kernel(even_ref, odd_ref, pre_ref, post_ref, high_ref, low_ref, out_ref, spec, shifted):
    g = pl.program_id(0)
    t = g // 2
    alternate = 1.0 - 2.0 * (lax.broadcasted_iota(jnp.int32, (8, BLOCK), 1) % 2).astype(F32)
    first = lax.broadcasted_iota(jnp.int32, (8, 128), 1) < 64

    def odd_block(plane, b):
        parts = []
        for h in range(2):
            zb = 4 * (b % 2) + 2 * h
            src = (plane * 8 + zb) * COLS + b // 2
            left = pltpu.roll(odd_ref[src], 64 * t, 1)
            right = pltpu.roll(odd_ref[src + COLS], 64 * (1 - t), 1)
            parts.append(jnp.where(first, left, right))
        return jnp.concatenate(parts, axis=1)

    for e in range(2):
        if e == 0:
            points = [tuple(even_ref[p, :, b * BLOCK : b * BLOCK + BLOCK] for p in range(2)) for b in range(RADIX)]
        else:
            points = [tuple(odd_block(p, b) for p in range(2)) for b in range(RADIX)]
        modes = dft16(points, -1)
        modes[0] = drop_half_mode(*modes[0], alternate)
        for k in range(RADIX):
            for p, value in enumerate(turn_by(*modes[k], pre_ref, k, slice(None))):
                for h in range(2):
                    rows = pl.ds(h * 512 + k * 32 + p * 16 + e, 8, stride=2)
                    spec[rows, :] = value[:, h * 128 : h * 128 + 128]
    for j in range(2):
        x = jnp.concatenate([spec[h * 512 + j * 256 : h * 512 + j * 256 + 256, :] for h in range(2)], axis=1)
        shifted[8 * j : 8 * j + 8] = product(x, high_ref[...], low_ref[...]).reshape(8, 32, 2 * BLOCK)
    for half in range(2):
        re_rows = slice(8 * half, 8 * half + 8)
        im_rows = slice(16 + 8 * half, 24 + 8 * half)

        @pl.loop(0, 4)
        def _(tile):
            lanes = pl.ds(pl.multiple_of(tile * 128, 128), 128)
            modes = [turn_by(shifted[k, re_rows, lanes], shifted[k, im_rows, lanes], post_ref, k, lanes) for k in range(RADIX)]
            values = dft16(modes, 1)
            for a in range(RADIX):
                where = pl.ds(pl.multiple_of(a * 2 * BLOCK + tile * 128, 128), 128)
                for p in range(2):
                    out_ref[p, re_rows, where] = values[a][p]


def on_device(velocity):
    old = np.arange(BLOCK, dtype=np.float64)
    lam = np.arange(BLOCK)
    order = 32 * ((lam % 128) // 16) + 16 * (lam // 128) + lam % 16
    both = np.arange(2 * BLOCK) / 2.0
    pre = phases(old, -1.0)
    post_y = phases(old[order] + 0.5, 1.0)
    post_z = phases(both, 1.0)
    high_y, low_y = split_bf16(shift_kernel(old[order] + 0.5))
    high_z, low_z = split_bf16(shift_kernel(both))
    vmem = pl.BlockSpec(memory_space=pltpu.VMEM)
    hbm = pl.BlockSpec(memory_space=pl.ANY)
    even, odd = pl.pallas_call(
        exchange_kernel,
        out_shape=(
            jax.ShapeDtypeStruct((2, 32, OLD_N), F32),
            jax.ShapeDtypeStruct((ROWS * COLS, 16, 128), F32),
        ),
        in_specs=[vmem] * 5,
        out_specs=(hbm, hbm),
        scratch_shapes=[
            pltpu.VMEM((ROWS, 64, BLOCK), F32),
            pltpu.VMEM((ROWS, 64, BLOCK), F32),
            pltpu.VMEM((RADIX, 64, BLOCK), F32),
            pltpu.VMEM((RADIX, 64, BLOCK), F32),
            pltpu.VMEM((RADIX, 2, 64, 128), F32),
            pltpu.VMEM((ROWS, 128, 128), F32),
            pltpu.VMEM((2, 256, 512), F32),
            pltpu.VMEM((8, 128), F32),
            pltpu.VMEM((ROWS, 8, 128), F32),
            pltpu.SemaphoreType.DMA((6,)),
            pltpu.SemaphoreType.DMA((4,)),
            pltpu.SemaphoreType.REGULAR,
        ],
        compiler_params=pltpu.CompilerParams(collective_id=0, has_side_effects=True, vmem_limit_bytes=48 << 20),
        name="exchange",
    )(velocity, jnp.asarray(pre), jnp.asarray(post_y), jnp.asarray(high_y), jnp.asarray(low_y))
    whole = lambda shape: pl.BlockSpec(shape, lambda g: (0,) * len(shape))
    return pl.pallas_call(
        refine_kernel,
        grid=(4,),
        out_shape=jax.ShapeDtypeStruct((2, 64, 2 * OLD_N), F32),
        in_specs=[
            pl.BlockSpec((2, 8, OLD_N), lambda g: (0, g, 0)),
            pl.BlockSpec((ROWS * COLS, 8, 128), lambda g: (0, g % 2, 0)),
            whole((2, RADIX, BLOCK)),
            whole((2, RADIX, 2 * BLOCK)),
            whole((BLOCK, 2 * BLOCK)),
            whole((BLOCK, 2 * BLOCK)),
        ],
        out_specs=pl.BlockSpec((2, 16, 2 * OLD_N), lambda g: (0, g, 0)),
        scratch_shapes=[
            pltpu.VMEM((1024, 128), F32),
            pltpu.VMEM((RADIX, 32, 2 * BLOCK), F32),
        ],
        compiler_params=pltpu.CompilerParams(vmem_limit_bytes=48 << 20),
        name="refine",
    )(even, odd, jnp.asarray(pre), jnp.asarray(post_z), jnp.asarray(high_z), jnp.asarray(low_z))


def solution(mesh):
    return jax.shard_map(
        on_device, mesh=mesh, in_specs=(P(None, "row", "col"),), out_specs=P(None, ("row", "col"), None), check_vma=False
    )
```

```python
import functools

import jax
import jax.numpy as jnp
import numpy as np
from jax import lax
from jax.experimental import pallas as pl
from jax.experimental.pallas import tpu as pltpu
from jax.sharding import PartitionSpec as P

OLD_N = 4096
RADIX = 16
BLOCK = 256
ROWS, COLS = 16, 8
MESH = pl.DeviceIdType.MESH
F32, BF16 = jnp.float32, jnp.bfloat16
PRE, POST_Y, POST_Z, TABLE_ROWS = 0, 64, 128, 256


def row_of(lam):
    return 32 * (lam % 128 // 16) + 16 * (lam // 128) + lam % 16


def fill_phases(table, base, tiles, halves, sign):
    for tile in range(tiles):
        k = lax.broadcasted_iota(jnp.int32, (RADIX, 128), 0) - RADIX // 2
        lane = lax.broadcasted_iota(jnp.int32, (RADIX, 128), 1) + tile * 128
        angle = (k * halves(lane)).astype(F32) * (sign * np.pi / OLD_N)
        table[base + tile * RADIX : base + tile * RADIX + RADIX, :] = jnp.cos(angle)
        table[base + (tiles + tile) * RADIX : base + (tiles + tile) * RADIX + RADIX, :] = jnp.sin(angle)


def fill_kernel(high, low, tiles, halves):
    for tile in range(tiles):

        @pl.loop(0, BLOCK // 32)
        def _(i):
            old = lax.broadcasted_iota(jnp.int32, (32, 128), 0) + i * 32
            twice = halves(lax.broadcasted_iota(jnp.int32, (32, 128), 1) + tile * 128) - 2 * old
            folded = jnp.where(twice > BLOCK, 2 * BLOCK - twice, jnp.where(twice < -BLOCK, -2 * BLOCK - twice, twice))
            odd = twice % 2 != 0
            sine = jnp.sin(jnp.where(odd, folded, 1).astype(F32) * (np.pi / (2 * BLOCK)))
            value = jnp.where((twice - 1) % 4 == 0, 1.0, -1.0) / (sine * (BLOCK * RADIX))
            value = jnp.where(odd, value, jnp.where(twice == 0, 1.0 / RADIX, 0.0))
            hi = value.astype(BF16)
            rows, lanes = pl.ds(pl.multiple_of(i * 32, 32), 32), slice(tile * 128, tile * 128 + 128)
            high[rows, lanes] = hi
            low[rows, lanes] = (value - hi.astype(F32)).astype(BF16)


def dft4(parts, sign):
    (ar, ai), (br, bi), (cr, ci), (dr, di) = parts
    sr, si, er, ei = ar + cr, ai + ci, ar - cr, ai - ci
    tr, ti, fr, fi = br + dr, bi + di, br - dr, bi - di
    if sign < 0:
        fr, fi = -fr, -fi
    return [(sr + tr, si + ti), (er - fi, ei + fr), (sr - tr, si - ti), (er + fi, ei - fr)]


def dft16(parts, sign):
    half = [dft4([parts[4 * hi + lo] for hi in range(4)], sign) for lo in range(4)]
    out = [None] * 16
    for klo in range(4):
        column = []
        for lo in range(4):
            re, im = half[lo][klo]
            turn = lo * klo
            if turn == 4:
                re, im = (-im, re) if sign > 0 else (im, -re)
            elif turn:
                c = float(np.cos(2 * np.pi * turn / 16))
                s = float(sign * np.sin(2 * np.pi * turn / 16))
                if turn == 2:
                    re, im = (re - im) * c if sign > 0 else (re + im) * c, (im + re) * c if sign > 0 else (im - re) * c
                elif turn == 6:
                    re, im = (re * c - im * s, re * s + im * c)
                else:
                    re, im = (re * c - im * s, re * s + im * c)
            column.append((re, im))
        for khi, value in enumerate(dft4(column, sign)):
            out[klo + 4 * khi] = value
    return out


def turn_by(re, im, table, base, tiles, tile, k):
    c = table[pl.ds(base + tile * RADIX + k, 1), :]
    s = table[pl.ds(base + (tiles + tile) * RADIX + k, 1), :]
    return re * c - im * s, re * s + im * c


def refine_rows(load, odd_row, table, high_ref, low_ref, spec, shifted, fine, finished=None):
    sign = 1.0 - 2.0 * (lax.broadcasted_iota(jnp.int32, (8, 128), 1) % 2).astype(F32)

    @pl.loop(0, 4)
    def _(g):
        first = []
        for h in range(2):
            modes = dft16([load(g, b, h) for b in range(RADIX)], -1)
            first.append(modes[0])
            for k in range(1, RADIX):
                for p, value in enumerate(turn_by(*modes[k], table, PRE, 2, h, k)):
                    spec[h, pl.ds(k * 64 + p * 32 + g * 8, 8), :] = value
        half = [
            sign * (jnp.sum((first[0][p] + first[1][p]) * sign, axis=-1, keepdims=True) * (1.0 / BLOCK)) for p in range(2)
        ]
        for h in range(2):
            for p, value in enumerate(turn_by(first[h][0] - half[0], first[h][1] - half[1], table, PRE, 2, h, 0)):
                spec[h, pl.ds(p * 32 + g * 8, 8), :] = value

    @pl.loop(0, 4)
    def _(j):
        rows = pl.ds(pl.multiple_of(j * 256, 256), 256)
        x = jnp.concatenate([spec[0, rows, :], spec[1, rows, :]], axis=1)
        shifted[rows, :] = product(x, high_ref[...], low_ref[...])

    @pl.loop(0, 4)
    def _(tile):
        lanes = pl.ds(pl.multiple_of(tile * 128, 128), 128)

        @pl.loop(0, 4)
        def _(g):
            modes = []
            for k in range(RADIX):
                re, im = (shifted[pl.ds(pl.multiple_of(k * 64 + p * 32 + g * 8, 8), 8), lanes] for p in range(2))
                modes.append(turn_by(re, im, table, POST_Z, 4, tile, k))
            values = dft16(modes, 1)
            for a in range(RADIX):
                for p in range(2):
                    fine[pl.ds(((p * RADIX + a) * 4 + tile) * 64 + g * 16 + odd_row, 8, stride=2), :] = values[a][p]

        if finished is not None:
            finished(tile)


def product(x, high, low):
    hi = x.astype(BF16)
    lo = (x - hi.astype(F32)).astype(BF16)
    dot = functools.partial(jnp.dot, preferred_element_type=F32)
    return dot(hi, high) + (dot(lo, high) + dot(hi, low))


def exchange_kernel(
    v_ref, fine, odd_ref, table, high_z, low_z, high_y, low_y, even_ref, spec_z, shifted_z,
    turned, lines, spec, shifted, back, outbox, fixed, sums, all_sums, send_sem, recv_sem, token,
):
    r, c = lax.axis_index("row"), lax.axis_index("col")

    def row_peer(i):
        return lax.rem(r + i, ROWS)

    def col_peer(i):
        return lax.rem(c + i, COLS)

    barrier = pltpu.get_barrier_semaphore()

    @pl.loop(1, ROWS)
    def _(i):
        pl.semaphore_signal(barrier, inc=1, device_id={"row": row_peer(i), "col": c}, device_id_type=MESH)

    @pl.loop(1, COLS)
    def _(i):
        pl.semaphore_signal(barrier, inc=1, device_id={"row": r, "col": col_peer(i)}, device_id_type=MESH)

    @pl.loop(0, 8)
    def _(q):
        plane, tile = q // 4, q % 4
        lanes = pl.ds(pl.multiple_of(tile * 128, 128), 128)
        for half in range(2):
            block = v_ref[plane, half * 128 : half * 128 + 128, lanes].T
            turned[2 * q, :, half * 128 : half * 128 + 128] = block[:64]
            turned[2 * q + 1, :, half * 128 : half * 128 + 128] = block[64:]

    sign8 = 1.0 - 2.0 * (lax.broadcasted_iota(jnp.int32, (8, 512), 0) % 2).astype(F32)
    for plane in range(2):
        total = jnp.zeros((8, 512), F32)
        for g in range(32):
            total = total + v_ref[plane, 8 * g : 8 * g + 8, :]
        total = jnp.sum(total * sign8, axis=0, keepdims=True)
        for tile in range(4):
            sums[plane * 4 + tile : plane * 4 + tile + 1, :] = total[:, tile * 128 : tile * 128 + 128]

    lines[r] = turned[r]
    all_sums[r] = sums[...]

    pl.semaphore_wait(barrier, ROWS + COLS - 2)

    @pl.loop(1, COLS)
    def _(i):
        pl.semaphore_signal(token, inc=1, device_id={"row": r, "col": col_peer(i)}, device_id_type=MESH)

    @pl.loop(1, ROWS)
    def _(i):
        pltpu.make_async_remote_copy(
            sums, all_sums.at[r], send_sem.at[1], recv_sem.at[1],
            device_id={"row": row_peer(i), "col": c}, device_id_type=MESH,
        ).start()

    @pl.loop(1, ROWS)
    def _(i):
        pltpu.make_async_remote_copy(
            turned.at[row_peer(i)], lines.at[r], send_sem.at[0], recv_sem.at[0],
            device_id={"row": row_peer(i), "col": c}, device_id_type=MESH,
        ).start()

    others = all_sums.at[pl.ds(0, ROWS - 1)]
    pltpu.make_async_copy(others, others, recv_sem.at[1]).wait()
    nyquist = all_sums[0]
    for i in range(1, ROWS):
        nyquist = nyquist + all_sums[i]
    nyquist = nyquist * (1.0 / OLD_N)
    for plane in range(2):
        row = jnp.concatenate([nyquist[plane * 4 + tile : plane * 4 + tile + 1] for tile in range(4)], axis=1)
        correction = row * sign8
        for g in range(32):
            fixed[plane, 8 * g : 8 * g + 8, :] = v_ref[plane, 8 * g : 8 * g + 8, :] - correction

    def old_rows(peer):
        return fixed.at[:, pl.ds(pl.multiple_of(peer * 32, 32), 32), :]

    my_columns = even_ref.at[:, :, pl.ds(pl.multiple_of(c * 512, 512), 512)]

    @pl.loop(1, COLS)
    def _(i):
        pltpu.make_async_remote_copy(
            old_rows(col_peer(i)), my_columns, send_sem.at[2], recv_sem.at[2],
            device_id={"row": r, "col": col_peer(i)}, device_id_type=MESH,
        ).start()

    own_even = pltpu.make_async_copy(old_rows(c), my_columns, send_sem.at[4])
    own_even.start()

    fill_phases(table, PRE, 2, lambda lane: 2 * lane, -1.0)
    fill_phases(table, POST_Y, 2, lambda lane: 2 * row_of(lane) + 1, 1.0)
    fill_phases(table, POST_Z, 4, lambda lane: lane, 1.0)
    fill_kernel(high_y, low_y, 2, lambda lane: 2 * row_of(lane) + 1)
    fill_kernel(high_z, low_z, 4, lambda lane: lane)

    others = lines.at[pl.ds(0, ROWS - 1)]
    pltpu.make_async_copy(others, others, recv_sem.at[0]).wait()

    sign = 1.0 - 2.0 * (lax.broadcasted_iota(jnp.int32, (8, 128), 1) % 2).astype(F32)

    @pl.loop(0, 4)
    def _(g):
        where = [pl.ds(pl.multiple_of(g * 8 + 32 * part, 8), 8) for part in range(2)]
        first = []
        for h in range(2):
            lanes = slice(h * 128, h * 128 + 128)
            modes = dft16([(lines[b, where[0], lanes], lines[b, where[1], lanes]) for b in range(RADIX)], -1)
            first.append(modes[0])
            for k in range(1, RADIX):
                for part, value in enumerate(turn_by(*modes[k], table, PRE, 2, h, k)):
                    spec[k, where[part], lanes] = value
        half = [
            sign * (jnp.sum((first[0][p] + first[1][p]) * sign, axis=-1, keepdims=True) * (1.0 / BLOCK)) for p in range(2)
        ]
        for h in range(2):
            lanes = slice(h * 128, h * 128 + 128)
            for part, value in enumerate(turn_by(first[h][0] - half[0], first[h][1] - half[1], table, PRE, 2, h, 0)):
                spec[0, where[part], lanes] = value

    @pl.loop(0, 4)
    def _(g):
        x = spec[pl.ds(g * 4, 4)].reshape(256, BLOCK)
        shifted[pl.ds(g * 4, 4)] = product(x, high_y[...], low_y[...]).reshape(4, 64, BLOCK)

    @pl.loop(0, 4)
    def _(g):
        where = [pl.ds(pl.multiple_of(g * 8 + 32 * part, 8), 8) for part in range(2)]
        for t in range(2):
            lanes = slice(t * 128, t * 128 + 128)
            modes = [
                turn_by(shifted[k, where[0], lanes], shifted[k, where[1], lanes], table, POST_Y, 2, t, k)
                for k in range(RADIX)
            ]
            points = dft16(modes, 1)
            for a in range(RADIX):
                for part in range(2):
                    back[a, t, where[part], :] = points[a][part]

    pl.semaphore_wait(token, COLS - 1)

    @pl.loop(0, ROWS)
    def _(i):
        a = row_peer(i)
        outbox[a] = back[a].reshape(128, 128).T

        @pl.loop(0, COLS)
        def _(j):
            peer = col_peer(j)

            @pl.when(i + j > 0)
            def _():
                pltpu.make_async_remote_copy(
                    outbox.at[a, pl.ds(pl.multiple_of(peer * 16, 16), 16), :], odd_ref.at[r * COLS + c],
                    send_sem.at[3], recv_sem.at[3],
                    device_id={"row": a, "col": peer}, device_id_type=MESH,
                ).start()

    own_odd = pltpu.make_async_copy(
        outbox.at[r, pl.ds(pl.multiple_of(c * 16, 16), 16), :], odd_ref.at[r * COLS + c], send_sem.at[5]
    )
    own_odd.start()

    own_even.wait()
    arrived = even_ref.at[:, :, pl.ds(0, 512 * (COLS - 1))]
    pltpu.make_async_copy(arrived, arrived, recv_sem.at[2]).wait()

    def load(g, b, h):
        rows = pl.ds(pl.multiple_of(g * 8, 8), 8)
        lanes = slice(b * BLOCK + h * 128, b * BLOCK + h * 128 + 128)
        return even_ref[0, rows, lanes], even_ref[1, rows, lanes]

    refine_rows(load, 0, table, high_z, low_z, spec_z, shifted_z, fine)

    own_odd.wait()
    sent = turned.at[pl.ds(0, ROWS - 1)]
    pltpu.make_async_copy(sent, sent, send_sem.at[0]).wait()
    sent = all_sums.at[pl.ds(0, ROWS - 1)]
    pltpu.make_async_copy(sent, sent, send_sem.at[1]).wait()
    sent = even_ref.at[:, :, pl.ds(0, 512 * (COLS - 1))]
    pltpu.make_async_copy(sent, sent, send_sem.at[2]).wait()
    sent = odd_ref.at[pl.ds(0, ROWS * COLS - 1)]
    pltpu.make_async_copy(sent, sent, send_sem.at[3]).wait()
    pltpu.make_async_copy(sent, sent, recv_sem.at[3]).wait()


def refine_kernel(fine_in, odd_ref, table, high_ref, low_ref, out_ref, fine, spec, shifted, sem):
    first = lax.broadcasted_iota(jnp.int32, (8, 128), 1) < 64

    def load(g, b, h):
        t, rows = g // 2, pl.ds(pl.multiple_of(8 * (g % 2), 8), 8)
        pair = []
        for plane in range(2):
            src = (plane * 8 + 4 * (b % 2) + 2 * h) * COLS + b // 2
            left = pltpu.roll(odd_ref[src, rows, :], 64 * t, 1)
            right = pltpu.roll(odd_ref[src + COLS, rows, :], 64 * (1 - t), 1)
            pair.append(jnp.where(first, left, right))
        return tuple(pair)

    def leave(tile):
        for p in range(2):

            @pl.loop(0, RADIX)
            def _(a):
                at = a * 4 + tile
                pltpu.make_async_copy(
                    fine.at[pl.ds(pl.multiple_of((p * 64 + at) * 64, 64), 64), :],
                    out_ref.at[p, :, pl.ds(pl.multiple_of(at * 128, 128), 128)],
                    sem,
                ).start()

    refine_rows(load, 1, table, high_ref, low_ref, spec, shifted, fine, leave)
    pltpu.make_async_copy(out_ref, out_ref, sem).wait()


def on_device(velocity):
    vmem = pl.BlockSpec(memory_space=pltpu.VMEM)
    hbm = pl.BlockSpec(memory_space=pltpu.HBM)
    fine, odd, phase, high, low = pl.pallas_call(
        exchange_kernel,
        out_shape=(
            jax.ShapeDtypeStruct((2 * 64 * 64, 128), F32),
            jax.ShapeDtypeStruct((ROWS * COLS, 16, 128), F32),
            jax.ShapeDtypeStruct((TABLE_ROWS, 128), F32),
            jax.ShapeDtypeStruct((BLOCK, 2 * BLOCK), BF16),
            jax.ShapeDtypeStruct((BLOCK, 2 * BLOCK), BF16),
        ),
        in_specs=[vmem],
        out_specs=(vmem,) * 5,
        scratch_shapes=[
            pltpu.VMEM((BLOCK, BLOCK), BF16),
            pltpu.VMEM((BLOCK, BLOCK), BF16),
            pltpu.VMEM((2, 32, OLD_N), F32),
            pltpu.VMEM((2, 1024, 128), F32),
            pltpu.VMEM((1024, 2 * BLOCK), F32),
            pltpu.VMEM((ROWS, 64, BLOCK), F32),
            pltpu.VMEM((ROWS, 64, BLOCK), F32),
            pltpu.VMEM((RADIX, 64, BLOCK), F32),
            pltpu.VMEM((RADIX, 64, BLOCK), F32),
            pltpu.VMEM((RADIX, 2, 64, 128), F32),
            pltpu.VMEM((ROWS, 128, 128), F32),
            pltpu.VMEM((2, 256, 512), F32),
            pltpu.VMEM((8, 128), F32),
            pltpu.VMEM((ROWS, 8, 128), F32),
            pltpu.SemaphoreType.DMA((8,)),
            pltpu.SemaphoreType.DMA((4,)),
            pltpu.SemaphoreType.REGULAR,
        ],
        compiler_params=pltpu.CompilerParams(collective_id=0, has_side_effects=True, vmem_limit_bytes=46 << 20),
        name="exchange",
    )(velocity)
    out, _ = pl.pallas_call(
        refine_kernel,
        out_shape=(
            jax.ShapeDtypeStruct((2, 64, 2 * OLD_N), F32),
            jax.ShapeDtypeStruct((2 * 64 * 64, 128), F32),
        ),
        in_specs=[vmem] * 5,
        out_specs=(hbm, vmem),
        scratch_shapes=[
            pltpu.VMEM((2, 1024, 128), F32),
            pltpu.VMEM((1024, 2 * BLOCK), F32),
            pltpu.SemaphoreType.DMA,
        ],
        input_output_aliases={0: 1},
        compiler_params=pltpu.CompilerParams(vmem_limit_bytes=40 << 20),
        name="refine",
    )(fine, odd, phase, high, low)
    return out


def solution(mesh):
    return jax.shard_map(
        on_device, mesh=mesh, in_specs=(P(None, "row", "col"),), out_specs=P(None, ("row", "col"), None), check_vma=False
    )
```

```python
import functools

import jax
import jax.numpy as jnp
import numpy as np
from jax import lax
from jax.experimental import pallas as pl
from jax.experimental.pallas import tpu as pltpu
from jax.sharding import PartitionSpec as P

OLD_N = 4096
RADIX = 16
BLOCK = 256
ROWS, COLS = 16, 8
MESH = pl.DeviceIdType.MESH
F32, BF16 = jnp.float32, jnp.bfloat16
PRE, POST_Y, POST_Z, TABLE_ROWS = 0, 64, 128, 256


def row_of(lam):
    return 32 * (lam % 128 // 16) + 16 * (lam // 128) + lam % 16


def fill_phases(table, base, tiles, halves, sign):
    for tile in range(tiles):
        k = lax.broadcasted_iota(jnp.int32, (RADIX, 128), 0) - RADIX // 2
        lane = lax.broadcasted_iota(jnp.int32, (RADIX, 128), 1) + tile * 128
        angle = (k * halves(lane)).astype(F32) * (sign * np.pi / OLD_N)
        table[base + tile * RADIX : base + tile * RADIX + RADIX, :] = jnp.cos(angle)
        table[base + (tiles + tile) * RADIX : base + (tiles + tile) * RADIX + RADIX, :] = jnp.sin(angle)


def fill_kernel(stacked, tiles, halves):
    for tile in range(tiles):

        @pl.loop(0, BLOCK // 32)
        def _(i):
            old = lax.broadcasted_iota(jnp.int32, (32, 128), 0) + i * 32
            twice = halves(lax.broadcasted_iota(jnp.int32, (32, 128), 1) + tile * 128) - 2 * old
            folded = jnp.where(twice > BLOCK, 2 * BLOCK - twice, jnp.where(twice < -BLOCK, -2 * BLOCK - twice, twice))
            odd = twice % 2 != 0
            sine = jnp.sin(jnp.where(odd, folded, 1).astype(F32) * (np.pi / (2 * BLOCK)))
            value = jnp.where((twice - 1) % 4 == 0, 1.0, -1.0) / (sine * (BLOCK * RADIX))
            value = jnp.where(odd, value, jnp.where(twice == 0, 1.0 / RADIX, 0.0))
            hi = value.astype(BF16)
            lanes = slice(tile * 128, tile * 128 + 128)
            for part, half in enumerate((hi, hi, (value - hi.astype(F32)).astype(BF16))):
                stacked[pl.ds(pl.multiple_of(part * BLOCK + i * 32, 32), 32), lanes] = half


def dft4(parts, sign):
    (ar, ai), (br, bi), (cr, ci), (dr, di) = parts
    sr, si, er, ei = ar + cr, ai + ci, ar - cr, ai - ci
    tr, ti, fr, fi = br + dr, bi + di, br - dr, bi - di
    if sign < 0:
        fr, fi = -fr, -fi
    return [(sr + tr, si + ti), (er - fi, ei + fr), (sr - tr, si - ti), (er + fi, ei - fr)]


def dft16(parts, sign):
    half = [dft4([parts[4 * hi + lo] for hi in range(4)], sign) for lo in range(4)]
    out = [None] * 16
    for klo in range(4):
        column = []
        for lo in range(4):
            re, im = half[lo][klo]
            turn = lo * klo
            if turn == 4:
                re, im = (-im, re) if sign > 0 else (im, -re)
            elif turn:
                c = float(np.cos(2 * np.pi * turn / 16))
                s = float(sign * np.sin(2 * np.pi * turn / 16))
                if turn == 2:
                    re, im = (re - im) * c if sign > 0 else (re + im) * c, (im + re) * c if sign > 0 else (im - re) * c
                elif turn == 6:
                    re, im = (re * c - im * s, re * s + im * c)
                else:
                    re, im = (re * c - im * s, re * s + im * c)
            column.append((re, im))
        for khi, value in enumerate(dft4(column, sign)):
            out[klo + 4 * khi] = value
    return out


def turn_by(re, im, table, base, tiles, tile, k):
    c = table[pl.ds(base + tile * RADIX + k, 1), :]
    s = table[pl.ds(base + (tiles + tile) * RADIX + k, 1), :]
    return re * c - im * s, re * s + im * c


def refine_rows(load, odd_row, table, stacked, spec, shifted, fine):
    sign = 1.0 - 2.0 * (lax.broadcasted_iota(jnp.int32, (8, 128), 1) % 2).astype(F32)

    @pl.loop(0, 4)
    def _(g):
        first = []
        for h in range(2):
            modes = dft16([load(g, b, h) for b in range(RADIX)], -1)
            first.append(modes[0])
            for k in range(1, RADIX):
                for p, value in enumerate(turn_by(*modes[k], table, PRE, 2, h, k)):
                    spec[h, pl.ds(k * 64 + p * 32 + g * 8, 8), :] = value
        half = [
            sign * (jnp.sum((first[0][p] + first[1][p]) * sign, axis=-1, keepdims=True) * (1.0 / BLOCK)) for p in range(2)
        ]
        for h in range(2):
            for p, value in enumerate(turn_by(first[h][0] - half[0], first[h][1] - half[1], table, PRE, 2, h, 0)):
                spec[h, pl.ds(p * 32 + g * 8, 8), :] = value

    @pl.loop(0, 4)
    def _(j):
        rows = pl.ds(pl.multiple_of(j * 256, 256), 256)
        x = jnp.concatenate([spec[0, rows, :], spec[1, rows, :]], axis=1)
        shifted[rows, :] = product(x, stacked)

    @pl.loop(0, 4)
    def _(tile):
        lanes = pl.ds(pl.multiple_of(tile * 128, 128), 128)

        @pl.loop(0, 4)
        def _(g):
            modes = []
            for k in range(RADIX):
                re, im = (shifted[pl.ds(pl.multiple_of(k * 64 + p * 32 + g * 8, 8), 8), lanes] for p in range(2))
                modes.append(turn_by(re, im, table, POST_Z, 4, tile, k))
            values = dft16(modes, 1)
            for a in range(RADIX):
                for p in range(2):
                    fine[pl.ds(((p * RADIX + a) * 4 + tile) * 64 + g * 16 + odd_row, 8, stride=2), :] = values[a][p]


def product(x, stacked):
    hi = x.astype(BF16)
    lo = (x - hi.astype(F32)).astype(BF16)
    return jnp.dot(jnp.concatenate([hi, lo, hi], axis=1), stacked[...], preferred_element_type=F32)


def exchange_kernel(
    v_ref, fine, odd_ref, table, kernel_z, kernel_y, even_ref, spec_z, shifted_z,
    turned, lines, spec, shifted, back, outbox, fixed, sums, all_sums, send_sem, recv_sem, token,
):
    r, c = lax.axis_index("row"), lax.axis_index("col")

    def row_peer(i):
        return lax.rem(r + i, ROWS)

    def col_peer(i):
        return lax.rem(c + i, COLS)

    barrier = pltpu.get_barrier_semaphore()

    @pl.loop(1, ROWS)
    def _(i):
        pl.semaphore_signal(barrier, inc=1, device_id={"row": row_peer(i), "col": c}, device_id_type=MESH)

    @pl.loop(1, COLS)
    def _(i):
        pl.semaphore_signal(barrier, inc=1, device_id={"row": r, "col": col_peer(i)}, device_id_type=MESH)

    @pl.loop(0, 8)
    def _(q):
        plane, tile = q // 4, q % 4
        lanes = pl.ds(pl.multiple_of(tile * 128, 128), 128)
        for half in range(2):
            block = v_ref[plane, half * 128 : half * 128 + 128, lanes].T
            turned[2 * q, :, half * 128 : half * 128 + 128] = block[:64]
            turned[2 * q + 1, :, half * 128 : half * 128 + 128] = block[64:]

    sign8 = 1.0 - 2.0 * (lax.broadcasted_iota(jnp.int32, (8, 512), 0) % 2).astype(F32)
    for plane in range(2):
        total = jnp.zeros((8, 512), F32)
        for g in range(32):
            total = total + v_ref[plane, 8 * g : 8 * g + 8, :]
        total = jnp.sum(total * sign8, axis=0, keepdims=True)
        for tile in range(4):
            sums[plane * 4 + tile : plane * 4 + tile + 1, :] = total[:, tile * 128 : tile * 128 + 128]

    lines[r] = turned[r]
    all_sums[r] = sums[...]

    pl.semaphore_wait(barrier, ROWS + COLS - 2)

    @pl.loop(1, COLS)
    def _(i):
        pl.semaphore_signal(token, inc=1, device_id={"row": r, "col": col_peer(i)}, device_id_type=MESH)

    @pl.loop(1, ROWS)
    def _(i):
        pltpu.make_async_remote_copy(
            sums, all_sums.at[r], send_sem.at[1], recv_sem.at[1],
            device_id={"row": row_peer(i), "col": c}, device_id_type=MESH,
        ).start()

    @pl.loop(1, ROWS)
    def _(i):
        pltpu.make_async_remote_copy(
            turned.at[row_peer(i)], lines.at[r], send_sem.at[0], recv_sem.at[0],
            device_id={"row": row_peer(i), "col": c}, device_id_type=MESH,
        ).start()

    others = all_sums.at[pl.ds(0, ROWS - 1)]
    pltpu.make_async_copy(others, others, recv_sem.at[1]).wait()
    nyquist = all_sums[0]
    for i in range(1, ROWS):
        nyquist = nyquist + all_sums[i]
    nyquist = nyquist * (1.0 / OLD_N)
    for plane in range(2):
        row = jnp.concatenate([nyquist[plane * 4 + tile : plane * 4 + tile + 1] for tile in range(4)], axis=1)
        correction = row * sign8
        for g in range(32):
            fixed[plane, 8 * g : 8 * g + 8, :] = v_ref[plane, 8 * g : 8 * g + 8, :] - correction

    def old_rows(peer):
        return fixed.at[:, pl.ds(pl.multiple_of(peer * 32, 32), 32), :]

    my_columns = even_ref.at[:, :, pl.ds(pl.multiple_of(c * 512, 512), 512)]

    @pl.loop(1, COLS)
    def _(i):
        pltpu.make_async_remote_copy(
            old_rows(col_peer(i)), my_columns, send_sem.at[2], recv_sem.at[2],
            device_id={"row": r, "col": col_peer(i)}, device_id_type=MESH,
        ).start()

    own_even = pltpu.make_async_copy(old_rows(c), my_columns, send_sem.at[4])
    own_even.start()

    fill_phases(table, PRE, 2, lambda lane: 2 * lane, -1.0)
    fill_phases(table, POST_Y, 2, lambda lane: 2 * row_of(lane) + 1, 1.0)
    fill_phases(table, POST_Z, 4, lambda lane: lane, 1.0)
    fill_kernel(kernel_y, 2, lambda lane: 2 * row_of(lane) + 1)
    fill_kernel(kernel_z, 4, lambda lane: lane)

    others = lines.at[pl.ds(0, ROWS - 1)]
    pltpu.make_async_copy(others, others, recv_sem.at[0]).wait()

    sign = 1.0 - 2.0 * (lax.broadcasted_iota(jnp.int32, (8, 128), 1) % 2).astype(F32)

    @pl.loop(0, 4)
    def _(g):
        where = [pl.ds(pl.multiple_of(g * 8 + 32 * part, 8), 8) for part in range(2)]
        first = []
        for h in range(2):
            lanes = slice(h * 128, h * 128 + 128)
            modes = dft16([(lines[b, where[0], lanes], lines[b, where[1], lanes]) for b in range(RADIX)], -1)
            first.append(modes[0])
            for k in range(1, RADIX):
                for part, value in enumerate(turn_by(*modes[k], table, PRE, 2, h, k)):
                    spec[k, where[part], lanes] = value
        half = [
            sign * (jnp.sum((first[0][p] + first[1][p]) * sign, axis=-1, keepdims=True) * (1.0 / BLOCK)) for p in range(2)
        ]
        for h in range(2):
            lanes = slice(h * 128, h * 128 + 128)
            for part, value in enumerate(turn_by(first[h][0] - half[0], first[h][1] - half[1], table, PRE, 2, h, 0)):
                spec[0, where[part], lanes] = value

    @pl.loop(0, 4)
    def _(g):
        x = spec[pl.ds(g * 4, 4)].reshape(256, BLOCK)
        shifted[pl.ds(g * 4, 4)] = product(x, kernel_y).reshape(4, 64, BLOCK)

    @pl.loop(0, 4)
    def _(g):
        where = [pl.ds(pl.multiple_of(g * 8 + 32 * part, 8), 8) for part in range(2)]
        for t in range(2):
            lanes = slice(t * 128, t * 128 + 128)
            modes = [
                turn_by(shifted[k, where[0], lanes], shifted[k, where[1], lanes], table, POST_Y, 2, t, k)
                for k in range(RADIX)
            ]
            points = dft16(modes, 1)
            for a in range(RADIX):
                for part in range(2):
                    back[a, t, where[part], :] = points[a][part]

    pl.semaphore_wait(token, COLS - 1)

    @pl.loop(0, ROWS)
    def _(i):
        a = row_peer(i)
        outbox[a] = back[a].reshape(128, 128).T

        @pl.loop(0, COLS)
        def _(j):
            peer = col_peer(j)

            @pl.when(i + j > 0)
            def _():
                pltpu.make_async_remote_copy(
                    outbox.at[a, pl.ds(pl.multiple_of(peer * 16, 16), 16), :], odd_ref.at[r * COLS + c],
                    send_sem.at[3], recv_sem.at[3],
                    device_id={"row": a, "col": peer}, device_id_type=MESH,
                ).start()

    own_odd = pltpu.make_async_copy(
        outbox.at[r, pl.ds(pl.multiple_of(c * 16, 16), 16), :], odd_ref.at[r * COLS + c], send_sem.at[5]
    )
    own_odd.start()

    own_even.wait()
    arrived = even_ref.at[:, :, pl.ds(0, 512 * (COLS - 1))]
    pltpu.make_async_copy(arrived, arrived, recv_sem.at[2]).wait()

    def load(g, b, h):
        rows = pl.ds(pl.multiple_of(g * 8, 8), 8)
        lanes = slice(b * BLOCK + h * 128, b * BLOCK + h * 128 + 128)
        return even_ref[0, rows, lanes], even_ref[1, rows, lanes]

    refine_rows(load, 0, table, kernel_z, spec_z, shifted_z, fine)

    own_odd.wait()
    sent = turned.at[pl.ds(0, ROWS - 1)]
    pltpu.make_async_copy(sent, sent, send_sem.at[0]).wait()
    sent = all_sums.at[pl.ds(0, ROWS - 1)]
    pltpu.make_async_copy(sent, sent, send_sem.at[1]).wait()
    sent = even_ref.at[:, :, pl.ds(0, 512 * (COLS - 1))]
    pltpu.make_async_copy(sent, sent, send_sem.at[2]).wait()
    sent = odd_ref.at[pl.ds(0, ROWS * COLS - 1)]
    pltpu.make_async_copy(sent, sent, send_sem.at[3]).wait()
    pltpu.make_async_copy(sent, sent, recv_sem.at[3]).wait()


def refine_kernel(fine_in, odd_ref, table, stacked, out_ref, fine, spec, shifted, sem):
    first = lax.broadcasted_iota(jnp.int32, (8, 128), 1) < 64
    sign = 1.0 - 2.0 * (lax.broadcasted_iota(jnp.int32, (8, 128), 1) % 2).astype(F32)
    by_tile = fine.reshape(2, 64, 8, 8, 128)

    def load(g, b, h):
        t, rows = g // 2, slice(8 * (g % 2), 8 * (g % 2) + 8)
        pair = []
        for plane in range(2):
            src = (plane * 8 + 4 * (b % 2) + 2 * h) * COLS + b // 2
            left, right = odd_ref[src, rows, :], odd_ref[src + COLS, rows, :]
            if t:
                left = pltpu.roll(left, 64, 1)
            else:
                right = pltpu.roll(right, 64, 1)
            pair.append(jnp.where(first, left, right))
        return tuple(pair)

    def to_modes(g):
        begin = []
        for h in range(2):
            modes = dft16([load(g, b, h) for b in range(RADIX)], -1)
            begin.append(modes[0])
            for k in range(1, RADIX):
                for p, value in enumerate(turn_by(*modes[k], table, PRE, 2, h, k)):
                    spec[g % 2, h, k * 16 + p * 8 : k * 16 + p * 8 + 8, :] = value
        half = [
            sign * (jnp.sum((begin[0][p] + begin[1][p]) * sign, axis=-1, keepdims=True) * (1.0 / BLOCK)) for p in range(2)
        ]
        for h in range(2):
            for p, value in enumerate(turn_by(begin[h][0] - half[0], begin[h][1] - half[1], table, PRE, 2, h, 0)):
                spec[g % 2, h, p * 8 : p * 8 + 8, :] = value

    def shift(g):
        x = jnp.concatenate([spec[g % 2, 0], spec[g % 2, 1]], axis=1)
        shifted[g % 2] = product(x, stacked)

    def to_points(g):
        for tile in range(4):
            lanes = slice(tile * 128, tile * 128 + 128)
            modes = []
            for k in range(RADIX):
                re, im = (shifted[g % 2, k * 16 + p * 8 : k * 16 + p * 8 + 8, lanes] for p in range(2))
                modes.append(turn_by(re, im, table, POST_Z, 4, tile, k))
            values = dft16(modes, 1)
            for a in range(RADIX):
                for p in range(2):
                    fine[pl.ds(((p * RADIX + a) * 4 + tile) * 64 + g * 16 + 1, 8, stride=2), :] = values[a][p]
        for p in range(2):
            for tile in (2 * g, 2 * g + 1):
                pltpu.make_async_copy(by_tile.at[p, :, tile], out_ref.at[p, tile], sem).start()

    for step in range(6):
        if step < 4:
            to_modes(step)
        if 1 <= step < 5:
            shift(step - 1)
        if step >= 2:
            to_points(step - 2)
    pltpu.make_async_copy(out_ref, out_ref, sem).wait()


def on_device(velocity):
    vmem = pl.BlockSpec(memory_space=pltpu.VMEM)
    hbm = pl.BlockSpec(memory_space=pltpu.HBM)
    fine, odd, phase, stacked = pl.pallas_call(
        exchange_kernel,
        out_shape=(
            jax.ShapeDtypeStruct((2 * 64 * 64, 128), F32),
            jax.ShapeDtypeStruct((ROWS * COLS, 16, 128), F32),
            jax.ShapeDtypeStruct((TABLE_ROWS, 128), F32),
            jax.ShapeDtypeStruct((3 * BLOCK, 2 * BLOCK), BF16),
        ),
        in_specs=[vmem],
        out_specs=(vmem,) * 4,
        scratch_shapes=[
            pltpu.VMEM((3 * BLOCK, BLOCK), BF16),
            pltpu.VMEM((2, 32, OLD_N), F32),
            pltpu.VMEM((2, 1024, 128), F32),
            pltpu.VMEM((1024, 2 * BLOCK), F32),
            pltpu.VMEM((ROWS, 64, BLOCK), F32),
            pltpu.VMEM((ROWS, 64, BLOCK), F32),
            pltpu.VMEM((RADIX, 64, BLOCK), F32),
            pltpu.VMEM((RADIX, 64, BLOCK), F32),
            pltpu.VMEM((RADIX, 2, 64, 128), F32),
            pltpu.VMEM((ROWS, 128, 128), F32),
            pltpu.VMEM((2, 256, 512), F32),
            pltpu.VMEM((8, 128), F32),
            pltpu.VMEM((ROWS, 8, 128), F32),
            pltpu.SemaphoreType.DMA((8,)),
            pltpu.SemaphoreType.DMA((4,)),
            pltpu.SemaphoreType.REGULAR,
        ],
        compiler_params=pltpu.CompilerParams(collective_id=0, has_side_effects=True, vmem_limit_bytes=46 << 20),
        name="exchange",
    )(velocity)
    out, _ = pl.pallas_call(
        refine_kernel,
        out_shape=(
            jax.ShapeDtypeStruct((2, 8, 64, 8, 128), F32),
            jax.ShapeDtypeStruct((2 * 64 * 64, 128), F32),
        ),
        in_specs=[vmem] * 4,
        out_specs=(hbm, vmem),
        scratch_shapes=[
            pltpu.VMEM((2, 2, 256, 128), F32),
            pltpu.VMEM((2, 256, 2 * BLOCK), F32),
            pltpu.SemaphoreType.DMA,
        ],
        input_output_aliases={0: 1},
        compiler_params=pltpu.CompilerParams(vmem_limit_bytes=40 << 20),
        name="refine",
    )(fine, odd, phase, stacked)
    return out.transpose(0, 1, 3, 2, 4).reshape(2, 64, 2 * OLD_N)


def solution(mesh):
    return jax.shard_map(
        on_device, mesh=mesh, in_specs=(P(None, "row", "col"),), out_specs=P(None, ("row", "col"), None), check_vma=False
    )
```

```python
import functools

import jax
import jax.numpy as jnp
import numpy as np
from jax import lax
from jax.experimental import pallas as pl
from jax.experimental.pallas import tpu as pltpu
from jax.sharding import PartitionSpec as P

OLD_N = 4096
RADIX = 16
BLOCK = 256
ROWS, COLS = 16, 8
MESH = pl.DeviceIdType.MESH
F32, BF16 = jnp.float32, jnp.bfloat16
PRE, POST_Y, POST_Z, TABLE_ROWS = 0, 64, 128, 256


def row_of(lam):
    return 32 * (lam % 128 // 16) + 16 * (lam // 128) + lam % 16


def fill_phases(table, base, tiles, halves, sign):
    for tile in range(tiles):
        k = lax.broadcasted_iota(jnp.int32, (RADIX, 128), 0) - RADIX // 2
        lane = lax.broadcasted_iota(jnp.int32, (RADIX, 128), 1) + tile * 128
        angle = (k * halves(lane)).astype(F32) * (sign * np.pi / OLD_N)
        table[base + tile * RADIX : base + tile * RADIX + RADIX, :] = jnp.cos(angle)
        table[base + (tiles + tile) * RADIX : base + (tiles + tile) * RADIX + RADIX, :] = jnp.sin(angle)


def fill_kernel(stacked, tiles, halves):
    for tile in range(tiles):

        @pl.loop(0, BLOCK // 32)
        def _(i):
            old = lax.broadcasted_iota(jnp.int32, (32, 128), 0) + i * 32
            twice = halves(lax.broadcasted_iota(jnp.int32, (32, 128), 1) + tile * 128) - 2 * old
            folded = jnp.where(twice > BLOCK, 2 * BLOCK - twice, jnp.where(twice < -BLOCK, -2 * BLOCK - twice, twice))
            odd = twice % 2 != 0
            sine = jnp.sin(jnp.where(odd, folded, 1).astype(F32) * (np.pi / (2 * BLOCK)))
            value = jnp.where((twice - 1) % 4 == 0, 1.0, -1.0) / (sine * (BLOCK * RADIX))
            value = jnp.where(odd, value, jnp.where(twice == 0, 1.0 / RADIX, 0.0))
            hi = value.astype(BF16)
            lanes = slice(tile * 128, tile * 128 + 128)
            for part, half in enumerate((hi, hi, (value - hi.astype(F32)).astype(BF16))):
                stacked[pl.ds(pl.multiple_of(part * BLOCK + i * 32, 32), 32), lanes] = half


def dft4(parts, sign):
    (ar, ai), (br, bi), (cr, ci), (dr, di) = parts
    sr, si, er, ei = ar + cr, ai + ci, ar - cr, ai - ci
    tr, ti, fr, fi = br + dr, bi + di, br - dr, bi - di
    if sign < 0:
        fr, fi = -fr, -fi
    return [(sr + tr, si + ti), (er - fi, ei + fr), (sr - tr, si - ti), (er + fi, ei - fr)]


def dft16(parts, sign):
    half = [dft4([parts[4 * hi + lo] for hi in range(4)], sign) for lo in range(4)]
    out = [None] * 16
    for klo in range(4):
        column = []
        for lo in range(4):
            re, im = half[lo][klo]
            turn = lo * klo
            if turn == 4:
                re, im = (-im, re) if sign > 0 else (im, -re)
            elif turn:
                c = float(np.cos(2 * np.pi * turn / 16))
                s = float(sign * np.sin(2 * np.pi * turn / 16))
                if turn == 2:
                    re, im = (re - im) * c if sign > 0 else (re + im) * c, (im + re) * c if sign > 0 else (im - re) * c
                elif turn == 6:
                    re, im = (re * c - im * s, re * s + im * c)
                else:
                    re, im = (re * c - im * s, re * s + im * c)
            column.append((re, im))
        for khi, value in enumerate(dft4(column, sign)):
            out[klo + 4 * khi] = value
    return out


def turn_by(re, im, table, base, tiles, tile, k):
    c = table[pl.ds(base + tile * RADIX + k, 1), :]
    s = table[pl.ds(base + (tiles + tile) * RADIX + k, 1), :]
    return re * c - im * s, re * s + im * c


def refine_rows(load, odd_row, table, stacked, spec, shifted, fine):
    sign = 1.0 - 2.0 * (lax.broadcasted_iota(jnp.int32, (8, 128), 1) % 2).astype(F32)

    @pl.loop(0, 4)
    def _(g):
        first = []
        for h in range(2):
            modes = dft16([load(g, b, h) for b in range(RADIX)], -1)
            first.append(modes[0])
            for k in range(1, RADIX):
                for p, value in enumerate(turn_by(*modes[k], table, PRE, 2, h, k)):
                    spec[h, pl.ds(k * 64 + p * 32 + g * 8, 8), :] = value
        half = [
            sign * (jnp.sum((first[0][p] + first[1][p]) * sign, axis=-1, keepdims=True) * (1.0 / BLOCK)) for p in range(2)
        ]
        for h in range(2):
            for p, value in enumerate(turn_by(first[h][0] - half[0], first[h][1] - half[1], table, PRE, 2, h, 0)):
                spec[h, pl.ds(p * 32 + g * 8, 8), :] = value

    @pl.loop(0, 4)
    def _(j):
        rows = pl.ds(pl.multiple_of(j * 256, 256), 256)
        x = jnp.concatenate([spec[0, rows, :], spec[1, rows, :]], axis=1)
        shifted[rows, :] = product(x, stacked)

    @pl.loop(0, 4)
    def _(tile):
        lanes = pl.ds(pl.multiple_of(tile * 128, 128), 128)

        @pl.loop(0, 4)
        def _(g):
            modes = []
            for k in range(RADIX):
                re, im = (shifted[pl.ds(pl.multiple_of(k * 64 + p * 32 + g * 8, 8), 8), lanes] for p in range(2))
                modes.append(turn_by(re, im, table, POST_Z, 4, tile, k))
            values = dft16(modes, 1)
            for a in range(RADIX):
                for p in range(2):
                    fine[pl.ds(((p * RADIX + a) * 4 + tile) * 64 + g * 16 + odd_row, 8, stride=2), :] = values[a][p]


def product(x, stacked):
    hi = x.astype(BF16)
    lo = (x - hi.astype(F32)).astype(BF16)
    return jnp.dot(jnp.concatenate([hi, lo, hi], axis=1), stacked[...], preferred_element_type=F32)


def exchange_kernel(
    v_ref, fine, odd_ref, table, kernel_z, kernel_y, even_ref, spec_z, shifted_z,
    turned, lines, spec, shifted, back, outbox, fixed, sums, all_sums, send_sem, recv_sem, token,
):
    r, c = lax.axis_index("row"), lax.axis_index("col")

    def row_peer(i):
        return lax.rem(r + i, ROWS)

    def col_peer(i):
        return lax.rem(c + i, COLS)

    barrier = pltpu.get_barrier_semaphore()

    @pl.loop(1, ROWS)
    def _(i):
        pl.semaphore_signal(barrier, inc=1, device_id={"row": row_peer(i), "col": c}, device_id_type=MESH)

    @pl.loop(1, COLS)
    def _(i):
        pl.semaphore_signal(barrier, inc=1, device_id={"row": r, "col": col_peer(i)}, device_id_type=MESH)

    @pl.loop(0, 8)
    def _(q):
        plane, tile = q // 4, q % 4
        lanes = pl.ds(pl.multiple_of(tile * 128, 128), 128)
        for half in range(2):
            block = v_ref[plane, half * 128 : half * 128 + 128, lanes].T
            turned[2 * q, :, half * 128 : half * 128 + 128] = block[:64]
            turned[2 * q + 1, :, half * 128 : half * 128 + 128] = block[64:]

    sign8 = 1.0 - 2.0 * (lax.broadcasted_iota(jnp.int32, (8, 512), 0) % 2).astype(F32)
    for plane in range(2):
        total = jnp.zeros((8, 512), F32)
        for g in range(32):
            total = total + v_ref[plane, 8 * g : 8 * g + 8, :]
        total = jnp.sum(total * sign8, axis=0, keepdims=True)
        for tile in range(4):
            sums[plane * 4 + tile : plane * 4 + tile + 1, :] = total[:, tile * 128 : tile * 128 + 128]

    lines[r] = turned[r]
    all_sums[r] = sums[...]

    pl.semaphore_wait(barrier, ROWS + COLS - 2)

    @pl.loop(1, COLS)
    def _(i):
        pl.semaphore_signal(token, inc=1, device_id={"row": r, "col": col_peer(i)}, device_id_type=MESH)

    @pl.loop(1, ROWS)
    def _(i):
        pltpu.make_async_remote_copy(
            sums, all_sums.at[r], send_sem.at[1], recv_sem.at[1],
            device_id={"row": row_peer(i), "col": c}, device_id_type=MESH,
        ).start()

    @pl.loop(1, ROWS)
    def _(i):
        pltpu.make_async_remote_copy(
            turned.at[row_peer(i)], lines.at[r], send_sem.at[0], recv_sem.at[0],
            device_id={"row": row_peer(i), "col": c}, device_id_type=MESH,
        ).start()

    others = all_sums.at[pl.ds(0, ROWS - 1)]
    pltpu.make_async_copy(others, others, recv_sem.at[1]).wait()
    nyquist = all_sums[0]
    for i in range(1, ROWS):
        nyquist = nyquist + all_sums[i]
    nyquist = nyquist * (1.0 / OLD_N)
    for plane in range(2):
        row = jnp.concatenate([nyquist[plane * 4 + tile : plane * 4 + tile + 1] for tile in range(4)], axis=1)
        correction = row * sign8
        for g in range(32):
            fixed[plane, 8 * g : 8 * g + 8, :] = v_ref[plane, 8 * g : 8 * g + 8, :] - correction

    def old_rows(peer):
        return fixed.at[:, pl.ds(pl.multiple_of(peer * 32, 32), 32), :]

    my_columns = even_ref.at[:, :, pl.ds(pl.multiple_of(c * 512, 512), 512)]

    @pl.loop(1, COLS)
    def _(i):
        pltpu.make_async_remote_copy(
            old_rows(col_peer(i)), my_columns, send_sem.at[2], recv_sem.at[2],
            device_id={"row": r, "col": col_peer(i)}, device_id_type=MESH,
        ).start()

    own_even = pltpu.make_async_copy(old_rows(c), my_columns, send_sem.at[4])
    own_even.start()

    fill_phases(table, PRE, 2, lambda lane: 2 * lane, -1.0)
    fill_phases(table, POST_Y, 2, lambda lane: 2 * row_of(lane) + 1, 1.0)
    fill_phases(table, POST_Z, 4, lambda lane: lane, 1.0)
    fill_kernel(kernel_y, 2, lambda lane: 2 * row_of(lane) + 1)
    fill_kernel(kernel_z, 4, lambda lane: lane)

    others = lines.at[pl.ds(0, ROWS - 1)]
    pltpu.make_async_copy(others, others, recv_sem.at[0]).wait()

    sign = 1.0 - 2.0 * (lax.broadcasted_iota(jnp.int32, (8, 128), 1) % 2).astype(F32)

    def to_modes(g):
        where = [slice(g * 8 + 32 * part, g * 8 + 32 * part + 8) for part in range(2)]
        first = []
        for h in range(2):
            lanes = slice(h * 128, h * 128 + 128)
            modes = dft16([(lines[b, where[0], lanes], lines[b, where[1], lanes]) for b in range(RADIX)], -1)
            first.append(modes[0])
            for k in range(1, RADIX):
                for part, value in enumerate(turn_by(*modes[k], table, PRE, 2, h, k)):
                    spec[g % 2, h, k * 16 + part * 8 : k * 16 + part * 8 + 8, :] = value
        half = [
            sign * (jnp.sum((first[0][p] + first[1][p]) * sign, axis=-1, keepdims=True) * (1.0 / BLOCK)) for p in range(2)
        ]
        for h in range(2):
            for part, value in enumerate(turn_by(first[h][0] - half[0], first[h][1] - half[1], table, PRE, 2, h, 0)):
                spec[g % 2, h, part * 8 : part * 8 + 8, :] = value

    def shift(g):
        shifted[g % 2] = product(jnp.concatenate([spec[g % 2, 0], spec[g % 2, 1]], axis=1), kernel_y)

    def to_points(g):
        for t in range(2):
            lanes = slice(t * 128, t * 128 + 128)
            modes = []
            for k in range(RADIX):
                re, im = (shifted[g % 2, k * 16 + part * 8 : k * 16 + part * 8 + 8, lanes] for part in range(2))
                modes.append(turn_by(re, im, table, POST_Y, 2, t, k))
            points = dft16(modes, 1)
            for a in range(RADIX):
                for part in range(2):
                    back[a, t, g * 8 + 32 * part : g * 8 + 32 * part + 8, :] = points[a][part]

    for step in range(6):
        if step < 4:
            to_modes(step)
        if 1 <= step < 5:
            shift(step - 1)
        if step >= 2:
            to_points(step - 2)

    pl.semaphore_wait(token, COLS - 1)

    @pl.loop(0, ROWS)
    def _(i):
        a = row_peer(i)
        outbox[a] = back[a].reshape(128, 128).T

        @pl.loop(0, COLS)
        def _(j):
            peer = col_peer(j)

            @pl.when(i + j > 0)
            def _():
                pltpu.make_async_remote_copy(
                    outbox.at[a, pl.ds(pl.multiple_of(peer * 16, 16), 16), :], odd_ref.at[r * COLS + c],
                    send_sem.at[3], recv_sem.at[3],
                    device_id={"row": a, "col": peer}, device_id_type=MESH,
                ).start()

    own_odd = pltpu.make_async_copy(
        outbox.at[r, pl.ds(pl.multiple_of(c * 16, 16), 16), :], odd_ref.at[r * COLS + c], send_sem.at[5]
    )
    own_odd.start()

    own_even.wait()
    arrived = even_ref.at[:, :, pl.ds(0, 512 * (COLS - 1))]
    pltpu.make_async_copy(arrived, arrived, recv_sem.at[2]).wait()

    def load(g, b, h):
        rows = pl.ds(pl.multiple_of(g * 8, 8), 8)
        lanes = slice(b * BLOCK + h * 128, b * BLOCK + h * 128 + 128)
        return even_ref[0, rows, lanes], even_ref[1, rows, lanes]

    refine_rows(load, 0, table, kernel_z, spec_z, shifted_z, fine)

    own_odd.wait()
    sent = turned.at[pl.ds(0, ROWS - 1)]
    pltpu.make_async_copy(sent, sent, send_sem.at[0]).wait()
    sent = all_sums.at[pl.ds(0, ROWS - 1)]
    pltpu.make_async_copy(sent, sent, send_sem.at[1]).wait()
    sent = even_ref.at[:, :, pl.ds(0, 512 * (COLS - 1))]
    pltpu.make_async_copy(sent, sent, send_sem.at[2]).wait()
    sent = odd_ref.at[pl.ds(0, ROWS * COLS - 1)]
    pltpu.make_async_copy(sent, sent, send_sem.at[3]).wait()
    pltpu.make_async_copy(sent, sent, recv_sem.at[3]).wait()


def refine_kernel(fine_in, odd_ref, table, stacked, out_ref, fine, spec, shifted, sem):
    first = lax.broadcasted_iota(jnp.int32, (8, 128), 1) < 64
    sign = 1.0 - 2.0 * (lax.broadcasted_iota(jnp.int32, (8, 128), 1) % 2).astype(F32)
    by_tile = fine.reshape(2, RADIX, 4, 8, 8, 128)

    def load(g, b, h):
        t, rows = g // 2, slice(8 * (g % 2), 8 * (g % 2) + 8)
        pair = []
        for plane in range(2):
            src = (plane * 8 + 4 * (b % 2) + 2 * h) * COLS + b // 2
            left, right = odd_ref[src, rows, :], odd_ref[src + COLS, rows, :]
            if t:
                left = pltpu.roll(left, 64, 1)
            else:
                right = pltpu.roll(right, 64, 1)
            pair.append(jnp.where(first, left, right))
        return tuple(pair)

    def to_modes(g):
        begin = []
        for h in range(2):
            modes = dft16([load(g, b, h) for b in range(RADIX)], -1)
            begin.append(modes[0])
            for k in range(1, RADIX):
                for p, value in enumerate(turn_by(*modes[k], table, PRE, 2, h, k)):
                    spec[g % 2, h, k * 16 + p * 8 : k * 16 + p * 8 + 8, :] = value
        half = [
            sign * (jnp.sum((begin[0][p] + begin[1][p]) * sign, axis=-1, keepdims=True) * (1.0 / BLOCK)) for p in range(2)
        ]
        for h in range(2):
            for p, value in enumerate(turn_by(begin[h][0] - half[0], begin[h][1] - half[1], table, PRE, 2, h, 0)):
                spec[g % 2, h, p * 8 : p * 8 + 8, :] = value

    def shift(g):
        x = jnp.concatenate([spec[g % 2, 0], spec[g % 2, 1]], axis=1)
        shifted[g % 2] = product(x, stacked)

    def to_points(g):
        for tile in range(4):
            lanes = slice(tile * 128, tile * 128 + 128)
            modes = []
            for k in range(RADIX):
                re, im = (shifted[g % 2, k * 16 + p * 8 : k * 16 + p * 8 + 8, lanes] for p in range(2))
                modes.append(turn_by(re, im, table, POST_Z, 4, tile, k))
            values = dft16(modes, 1)
            for a in range(RADIX):
                for p in range(2):
                    fine[pl.ds(((p * RADIX + a) * 4 + tile) * 64 + g * 16 + 1, 8, stride=2), :] = values[a][p]
            for p in range(2):
                for eight in (2 * g, 2 * g + 1):
                    pltpu.make_async_copy(by_tile.at[p, :, tile, eight], out_ref.at[p, eight, :, tile], sem).start()

    for step in range(6):
        if step < 4:
            to_modes(step)
        if 1 <= step < 5:
            shift(step - 1)
        if step >= 2:
            to_points(step - 2)
    pltpu.make_async_copy(out_ref, out_ref, sem).wait()


def on_device(velocity):
    vmem = pl.BlockSpec(memory_space=pltpu.VMEM)
    hbm = pl.BlockSpec(memory_space=pltpu.HBM)
    fine, odd, phase, stacked = pl.pallas_call(
        exchange_kernel,
        out_shape=(
            jax.ShapeDtypeStruct((2 * 64 * 64, 128), F32),
            jax.ShapeDtypeStruct((ROWS * COLS, 16, 128), F32),
            jax.ShapeDtypeStruct((TABLE_ROWS, 128), F32),
            jax.ShapeDtypeStruct((3 * BLOCK, 2 * BLOCK), BF16),
        ),
        in_specs=[vmem],
        out_specs=(vmem,) * 4,
        scratch_shapes=[
            pltpu.VMEM((3 * BLOCK, BLOCK), BF16),
            pltpu.VMEM((2, 32, OLD_N), F32),
            pltpu.VMEM((2, 1024, 128), F32),
            pltpu.VMEM((1024, 2 * BLOCK), F32),
            pltpu.VMEM((ROWS, 64, BLOCK), F32),
            pltpu.VMEM((ROWS, 64, BLOCK), F32),
            pltpu.VMEM((2, 2, 256, 128), F32),
            pltpu.VMEM((2, 256, BLOCK), F32),
            pltpu.VMEM((RADIX, 2, 64, 128), F32),
            pltpu.VMEM((ROWS, 128, 128), F32),
            pltpu.VMEM((2, 256, 512), F32),
            pltpu.VMEM((8, 128), F32),
            pltpu.VMEM((ROWS, 8, 128), F32),
            pltpu.SemaphoreType.DMA((8,)),
            pltpu.SemaphoreType.DMA((4,)),
            pltpu.SemaphoreType.REGULAR,
        ],
        compiler_params=pltpu.CompilerParams(collective_id=0, has_side_effects=True, vmem_limit_bytes=46 << 20),
        name="exchange",
    )(velocity)
    out, _ = pl.pallas_call(
        refine_kernel,
        out_shape=(
            jax.ShapeDtypeStruct((2, 8, RADIX, 4, 8, 128), F32),
            jax.ShapeDtypeStruct((2 * 64 * 64, 128), F32),
        ),
        in_specs=[vmem] * 4,
        out_specs=(hbm, vmem),
        scratch_shapes=[
            pltpu.VMEM((2, 2, 256, 128), F32),
            pltpu.VMEM((2, 256, 2 * BLOCK), F32),
            pltpu.SemaphoreType.DMA,
        ],
        input_output_aliases={0: 1},
        compiler_params=pltpu.CompilerParams(vmem_limit_bytes=40 << 20),
        name="refine",
    )(fine, odd, phase, stacked)
    return out.reshape(2, 8, 64, 8, 128).transpose(0, 1, 3, 2, 4).reshape(2, 64, 2 * OLD_N)


def solution(mesh):
    return jax.shard_map(
        on_device, mesh=mesh, in_specs=(P(None, "row", "col"),), out_specs=P(None, ("row", "col"), None), check_vma=False
    )
```

```python
import functools

import jax
import jax.numpy as jnp
import numpy as np
from jax import lax
from jax.experimental import pallas as pl
from jax.experimental.pallas import tpu as pltpu
from jax.sharding import PartitionSpec as P

OLD_N = 4096
RADIX = 16
BLOCK = 256
ROWS, COLS = 16, 8
MESH = pl.DeviceIdType.MESH
F32, BF16 = jnp.float32, jnp.bfloat16
PRE, POST_Y, POST_Z, TABLE_ROWS = 0, 64, 128, 256


def row_of(lam):
    return 32 * (lam % 128 // 16) + 16 * (lam // 128) + lam % 16


def fill_phases(table, base, tiles, halves, sign):
    for tile in range(tiles):
        k = lax.broadcasted_iota(jnp.int32, (RADIX, 128), 0) - RADIX // 2
        lane = lax.broadcasted_iota(jnp.int32, (RADIX, 128), 1) + tile * 128
        angle = (k * halves(lane)).astype(F32) * (sign * np.pi / OLD_N)
        table[base + tile * RADIX : base + tile * RADIX + RADIX, :] = jnp.cos(angle)
        table[base + (tiles + tile) * RADIX : base + (tiles + tile) * RADIX + RADIX, :] = jnp.sin(angle)


def fill_kernel(stacked, tiles, halves):
    for tile in range(tiles):

        @pl.loop(0, BLOCK // 32)
        def _(i):
            old = lax.broadcasted_iota(jnp.int32, (32, 128), 0) + i * 32
            twice = halves(lax.broadcasted_iota(jnp.int32, (32, 128), 1) + tile * 128) - 2 * old
            folded = jnp.where(twice > BLOCK, 2 * BLOCK - twice, jnp.where(twice < -BLOCK, -2 * BLOCK - twice, twice))
            odd = twice % 2 != 0
            sine = jnp.sin(jnp.where(odd, folded, 1).astype(F32) * (np.pi / (2 * BLOCK)))
            value = jnp.where((twice - 1) % 4 == 0, 1.0, -1.0) / (sine * (BLOCK * RADIX))
            value = jnp.where(odd, value, jnp.where(twice == 0, 1.0 / RADIX, 0.0))
            hi = value.astype(BF16)
            lanes = slice(tile * 128, tile * 128 + 128)
            for part, half in enumerate((hi, hi, (value - hi.astype(F32)).astype(BF16))):
                stacked[pl.ds(pl.multiple_of(part * BLOCK + i * 32, 32), 32), lanes] = half


def dft4(parts, sign):
    (ar, ai), (br, bi), (cr, ci), (dr, di) = parts
    sr, si, er, ei = ar + cr, ai + ci, ar - cr, ai - ci
    tr, ti, fr, fi = br + dr, bi + di, br - dr, bi - di
    if sign < 0:
        fr, fi = -fr, -fi
    return [(sr + tr, si + ti), (er - fi, ei + fr), (sr - tr, si - ti), (er + fi, ei - fr)]


def dft16(parts, sign):
    half = [dft4([parts[4 * hi + lo] for hi in range(4)], sign) for lo in range(4)]
    out = [None] * 16
    for klo in range(4):
        column = []
        for lo in range(4):
            re, im = half[lo][klo]
            turn = lo * klo
            if turn == 4:
                re, im = (-im, re) if sign > 0 else (im, -re)
            elif turn:
                c = float(np.cos(2 * np.pi * turn / 16))
                s = float(sign * np.sin(2 * np.pi * turn / 16))
                if turn == 2:
                    re, im = (re - im) * c if sign > 0 else (re + im) * c, (im + re) * c if sign > 0 else (im - re) * c
                elif turn == 6:
                    re, im = (re * c - im * s, re * s + im * c)
                else:
                    re, im = (re * c - im * s, re * s + im * c)
            column.append((re, im))
        for khi, value in enumerate(dft4(column, sign)):
            out[klo + 4 * khi] = value
    return out


def turn_by(re, im, table, base, tiles, tile, k):
    c = table[pl.ds(base + tile * RADIX + k, 1), :]
    s = table[pl.ds(base + (tiles + tile) * RADIX + k, 1), :]
    return re * c - im * s, re * s + im * c


def refine_rows(load, odd_row, table, stacked, spec, shifted, fine):
    sign = 1.0 - 2.0 * (lax.broadcasted_iota(jnp.int32, (8, 128), 1) % 2).astype(F32)

    @pl.loop(0, 4)
    def _(g):
        first = []
        for h in range(2):
            modes = dft16([load(g, b, h) for b in range(RADIX)], -1)
            first.append(modes[0])
            for k in range(1, RADIX):
                for p, value in enumerate(turn_by(*modes[k], table, PRE, 2, h, k)):
                    spec[h, pl.ds(k * 64 + p * 32 + g * 8, 8), :] = value
        half = [
            sign * (jnp.sum((first[0][p] + first[1][p]) * sign, axis=-1, keepdims=True) * (1.0 / BLOCK)) for p in range(2)
        ]
        for h in range(2):
            for p, value in enumerate(turn_by(first[h][0] - half[0], first[h][1] - half[1], table, PRE, 2, h, 0)):
                spec[h, pl.ds(p * 32 + g * 8, 8), :] = value

    @pl.loop(0, 4)
    def _(j):
        rows = pl.ds(pl.multiple_of(j * 256, 256), 256)
        x = jnp.concatenate([spec[0, rows, :], spec[1, rows, :]], axis=1)
        shifted[rows, :] = product(x, stacked)

    @pl.loop(0, 4)
    def _(tile):
        lanes = pl.ds(pl.multiple_of(tile * 128, 128), 128)

        @pl.loop(0, 4)
        def _(g):
            modes = []
            for k in range(RADIX):
                re, im = (shifted[pl.ds(pl.multiple_of(k * 64 + p * 32 + g * 8, 8), 8), lanes] for p in range(2))
                modes.append(turn_by(re, im, table, POST_Z, 4, tile, k))
            values = dft16(modes, 1)
            for a in range(RADIX):
                for p in range(2):
                    fine[pl.ds(((p * RADIX + a) * 4 + tile) * 64 + g * 16 + odd_row, 8, stride=2), :] = values[a][p]


def product(x, stacked):
    hi = x.astype(BF16)
    lo = (x - hi.astype(F32)).astype(BF16)
    return jnp.dot(jnp.concatenate([hi, lo, hi], axis=1), stacked[...], preferred_element_type=F32)


def exchange_kernel(
    v_ref, fine, odd_ref, table, kernel_z, kernel_y, even_ref, spec_z, shifted_z,
    turned, lines, spec, shifted, back, outbox, fixed, sums, all_sums, send_sem, recv_sem, token,
):
    r, c = lax.axis_index("row"), lax.axis_index("col")

    def row_peer(i):
        return lax.rem(r + i, ROWS)

    def col_peer(i):
        return lax.rem(c + i, COLS)

    barrier = pltpu.get_barrier_semaphore()

    @pl.loop(1, ROWS)
    def _(i):
        pl.semaphore_signal(barrier, inc=1, device_id={"row": row_peer(i), "col": c}, device_id_type=MESH)

    @pl.loop(1, COLS)
    def _(i):
        pl.semaphore_signal(barrier, inc=1, device_id={"row": r, "col": col_peer(i)}, device_id_type=MESH)

    @pl.loop(0, 8)
    def _(q):
        plane, tile = q // 4, q % 4
        lanes = pl.ds(pl.multiple_of(tile * 128, 128), 128)
        for half in range(2):
            block = v_ref[plane, half * 128 : half * 128 + 128, lanes].T
            turned[2 * q, :, half * 128 : half * 128 + 128] = block[:64]
            turned[2 * q + 1, :, half * 128 : half * 128 + 128] = block[64:]

    sign8 = 1.0 - 2.0 * (lax.broadcasted_iota(jnp.int32, (8, 512), 0) % 2).astype(F32)
    for plane in range(2):
        total = jnp.zeros((8, 512), F32)
        for g in range(32):
            total = total + v_ref[plane, 8 * g : 8 * g + 8, :]
        total = jnp.sum(total * sign8, axis=0, keepdims=True)
        for tile in range(4):
            sums[plane * 4 + tile : plane * 4 + tile + 1, :] = total[:, tile * 128 : tile * 128 + 128]

    lines[r] = turned[r]
    all_sums[r] = sums[...]

    pl.semaphore_wait(barrier, ROWS + COLS - 2)

    @pl.loop(1, ROWS)
    def _(i):
        pltpu.make_async_remote_copy(
            sums, all_sums.at[r], send_sem.at[1], recv_sem.at[1],
            device_id={"row": row_peer(i), "col": c}, device_id_type=MESH,
        ).start()

    @pl.loop(0, ROWS - 1)
    def _(i):
        half = lax.rem(r // 8 + 1 + lax.rem(i, 2), 2)
        owner = half * 8 + lax.rem(r + (i + 1) // 2, 8)
        pltpu.make_async_remote_copy(
            turned.at[owner], lines.at[r], send_sem.at[0], recv_sem.at[0],
            device_id={"row": owner, "col": c}, device_id_type=MESH,
        ).start()

    @pl.loop(1, COLS)
    def _(i):
        pl.semaphore_signal(token, inc=1, device_id={"row": r, "col": col_peer(i)}, device_id_type=MESH)

    others = all_sums.at[pl.ds(0, ROWS - 1)]
    pltpu.make_async_copy(others, others, recv_sem.at[1]).wait()
    nyquist = all_sums[0]
    for i in range(1, ROWS):
        nyquist = nyquist + all_sums[i]
    nyquist = nyquist * (1.0 / OLD_N)
    for plane in range(2):
        row = jnp.concatenate([nyquist[plane * 4 + tile : plane * 4 + tile + 1] for tile in range(4)], axis=1)
        correction = row * sign8
        for g in range(32):
            fixed[plane, 8 * g : 8 * g + 8, :] = v_ref[plane, 8 * g : 8 * g + 8, :] - correction

    def old_rows(peer):
        return fixed.at[:, pl.ds(pl.multiple_of(peer * 32, 32), 32), :]

    my_columns = even_ref.at[:, :, pl.ds(pl.multiple_of(c * 512, 512), 512)]

    @pl.loop(1, COLS)
    def _(i):
        pltpu.make_async_remote_copy(
            old_rows(col_peer(i)), my_columns, send_sem.at[2], recv_sem.at[2],
            device_id={"row": r, "col": col_peer(i)}, device_id_type=MESH,
        ).start()

    own_even = pltpu.make_async_copy(old_rows(c), my_columns, send_sem.at[4])
    own_even.start()

    fill_phases(table, PRE, 2, lambda lane: 2 * lane, -1.0)
    fill_phases(table, POST_Y, 2, lambda lane: 2 * row_of(lane) + 1, 1.0)
    fill_phases(table, POST_Z, 4, lambda lane: lane, 1.0)
    fill_kernel(kernel_y, 2, lambda lane: 2 * row_of(lane) + 1)
    fill_kernel(kernel_z, 4, lambda lane: lane)

    others = lines.at[pl.ds(0, ROWS - 1)]
    pltpu.make_async_copy(others, others, recv_sem.at[0]).wait()

    sign = 1.0 - 2.0 * (lax.broadcasted_iota(jnp.int32, (8, 128), 1) % 2).astype(F32)

    def to_modes(g):
        where = [slice(g * 8 + 32 * part, g * 8 + 32 * part + 8) for part in range(2)]
        first = []
        for h in range(2):
            lanes = slice(h * 128, h * 128 + 128)
            modes = dft16([(lines[b, where[0], lanes], lines[b, where[1], lanes]) for b in range(RADIX)], -1)
            first.append(modes[0])
            for k in range(1, RADIX):
                for part, value in enumerate(turn_by(*modes[k], table, PRE, 2, h, k)):
                    spec[g % 2, h, k * 16 + part * 8 : k * 16 + part * 8 + 8, :] = value
        half = [
            sign * (jnp.sum((first[0][p] + first[1][p]) * sign, axis=-1, keepdims=True) * (1.0 / BLOCK)) for p in range(2)
        ]
        for h in range(2):
            for part, value in enumerate(turn_by(first[h][0] - half[0], first[h][1] - half[1], table, PRE, 2, h, 0)):
                spec[g % 2, h, part * 8 : part * 8 + 8, :] = value

    def shift(g):
        shifted[g % 2] = product(jnp.concatenate([spec[g % 2, 0], spec[g % 2, 1]], axis=1), kernel_y)

    def to_points(g):
        for t in range(2):
            lanes = slice(t * 128, t * 128 + 128)
            modes = []
            for k in range(RADIX):
                re, im = (shifted[g % 2, k * 16 + part * 8 : k * 16 + part * 8 + 8, lanes] for part in range(2))
                modes.append(turn_by(re, im, table, POST_Y, 2, t, k))
            points = dft16(modes, 1)
            for a in range(RADIX):
                for part in range(2):
                    back[a, t, g * 8 + 32 * part : g * 8 + 32 * part + 8, :] = points[a][part]

    for step in range(6):
        if step < 4:
            to_modes(step)
        if 1 <= step < 5:
            shift(step - 1)
        if step >= 2:
            to_points(step - 2)

    pl.semaphore_wait(token, COLS - 1)

    @pl.loop(0, ROWS)
    def _(i):
        a = row_peer(i)
        outbox[a] = back[a].reshape(128, 128).T

        @pl.loop(0, COLS)
        def _(j):
            peer = col_peer(j)

            @pl.when(i + j > 0)
            def _():
                pltpu.make_async_remote_copy(
                    outbox.at[a, pl.ds(pl.multiple_of(peer * 16, 16), 16), :], odd_ref.at[r * COLS + c],
                    send_sem.at[3], recv_sem.at[3],
                    device_id={"row": a, "col": peer}, device_id_type=MESH,
                ).start()

    own_odd = pltpu.make_async_copy(
        outbox.at[r, pl.ds(pl.multiple_of(c * 16, 16), 16), :], odd_ref.at[r * COLS + c], send_sem.at[5]
    )
    own_odd.start()

    own_even.wait()
    arrived = even_ref.at[:, :, pl.ds(0, 512 * (COLS - 1))]
    pltpu.make_async_copy(arrived, arrived, recv_sem.at[2]).wait()

    def load(g, b, h):
        rows = pl.ds(pl.multiple_of(g * 8, 8), 8)
        lanes = slice(b * BLOCK + h * 128, b * BLOCK + h * 128 + 128)
        return even_ref[0, rows, lanes], even_ref[1, rows, lanes]

    refine_rows(load, 0, table, kernel_z, spec_z, shifted_z, fine)

    own_odd.wait()
    sent = turned.at[pl.ds(0, ROWS - 1)]
    pltpu.make_async_copy(sent, sent, send_sem.at[0]).wait()
    sent = all_sums.at[pl.ds(0, ROWS - 1)]
    pltpu.make_async_copy(sent, sent, send_sem.at[1]).wait()
    sent = even_ref.at[:, :, pl.ds(0, 512 * (COLS - 1))]
    pltpu.make_async_copy(sent, sent, send_sem.at[2]).wait()
    sent = odd_ref.at[pl.ds(0, ROWS * COLS - 1)]
    pltpu.make_async_copy(sent, sent, send_sem.at[3]).wait()
    pltpu.make_async_copy(sent, sent, recv_sem.at[3]).wait()


def refine_kernel(fine_in, odd_ref, table, stacked, out_ref, fine, spec, shifted, sem):
    first = lax.broadcasted_iota(jnp.int32, (8, 128), 1) < 64
    sign = 1.0 - 2.0 * (lax.broadcasted_iota(jnp.int32, (8, 128), 1) % 2).astype(F32)
    by_tile = fine.reshape(2, RADIX, 4, 8, 8, 128)

    def load(g, b, h):
        t, rows = g // 2, slice(8 * (g % 2), 8 * (g % 2) + 8)
        pair = []
        for plane in range(2):
            src = (plane * 8 + 4 * (b % 2) + 2 * h) * COLS + b // 2
            left, right = odd_ref[src, rows, :], odd_ref[src + COLS, rows, :]
            if t:
                left = pltpu.roll(left, 64, 1)
            else:
                right = pltpu.roll(right, 64, 1)
            pair.append(jnp.where(first, left, right))
        return tuple(pair)

    def to_modes(g):
        begin = []
        for h in range(2):
            modes = dft16([load(g, b, h) for b in range(RADIX)], -1)
            begin.append(modes[0])
            for k in range(1, RADIX):
                for p, value in enumerate(turn_by(*modes[k], table, PRE, 2, h, k)):
                    spec[g % 2, h, k * 16 + p * 8 : k * 16 + p * 8 + 8, :] = value
        half = [
            sign * (jnp.sum((begin[0][p] + begin[1][p]) * sign, axis=-1, keepdims=True) * (1.0 / BLOCK)) for p in range(2)
        ]
        for h in range(2):
            for p, value in enumerate(turn_by(begin[h][0] - half[0], begin[h][1] - half[1], table, PRE, 2, h, 0)):
                spec[g % 2, h, p * 8 : p * 8 + 8, :] = value

    def shift(g):
        x = jnp.concatenate([spec[g % 2, 0], spec[g % 2, 1]], axis=1)
        shifted[g % 2] = product(x, stacked)

    def to_points(g):
        for tile in range(4):
            lanes = slice(tile * 128, tile * 128 + 128)
            modes = []
            for k in range(RADIX):
                re, im = (shifted[g % 2, k * 16 + p * 8 : k * 16 + p * 8 + 8, lanes] for p in range(2))
                modes.append(turn_by(re, im, table, POST_Z, 4, tile, k))
            values = dft16(modes, 1)
            for a in range(RADIX):
                for p in range(2):
                    fine[pl.ds(((p * RADIX + a) * 4 + tile) * 64 + g * 16 + 1, 8, stride=2), :] = values[a][p]
            for p in range(2):
                for eight in (2 * g, 2 * g + 1):
                    pltpu.make_async_copy(by_tile.at[p, :, tile, eight], out_ref.at[p, eight, :, tile], sem).start()

    for step in range(6):
        if step < 4:
            to_modes(step)
        if 1 <= step < 5:
            shift(step - 1)
        if step >= 2:
            to_points(step - 2)
    pltpu.make_async_copy(out_ref, out_ref, sem).wait()


def on_device(velocity):
    vmem = pl.BlockSpec(memory_space=pltpu.VMEM)
    hbm = pl.BlockSpec(memory_space=pltpu.HBM)
    fine, odd, phase, stacked = pl.pallas_call(
        exchange_kernel,
        out_shape=(
            jax.ShapeDtypeStruct((2 * 64 * 64, 128), F32),
            jax.ShapeDtypeStruct((ROWS * COLS, 16, 128), F32),
            jax.ShapeDtypeStruct((TABLE_ROWS, 128), F32),
            jax.ShapeDtypeStruct((3 * BLOCK, 2 * BLOCK), BF16),
        ),
        in_specs=[vmem],
        out_specs=(vmem,) * 4,
        scratch_shapes=[
            pltpu.VMEM((3 * BLOCK, BLOCK), BF16),
            pltpu.VMEM((2, 32, OLD_N), F32),
            pltpu.VMEM((2, 1024, 128), F32),
            pltpu.VMEM((1024, 2 * BLOCK), F32),
            pltpu.VMEM((ROWS, 64, BLOCK), F32),
            pltpu.VMEM((ROWS, 64, BLOCK), F32),
            pltpu.VMEM((2, 2, 256, 128), F32),
            pltpu.VMEM((2, 256, BLOCK), F32),
            pltpu.VMEM((RADIX, 2, 64, 128), F32),
            pltpu.VMEM((ROWS, 128, 128), F32),
            pltpu.VMEM((2, 256, 512), F32),
            pltpu.VMEM((8, 128), F32),
            pltpu.VMEM((ROWS, 8, 128), F32),
            pltpu.SemaphoreType.DMA((8,)),
            pltpu.SemaphoreType.DMA((4,)),
            pltpu.SemaphoreType.REGULAR,
        ],
        compiler_params=pltpu.CompilerParams(collective_id=0, has_side_effects=True, vmem_limit_bytes=46 << 20),
        name="exchange",
    )(velocity)
    out, _ = pl.pallas_call(
        refine_kernel,
        out_shape=(
            jax.ShapeDtypeStruct((2, 8, RADIX, 4, 8, 128), F32),
            jax.ShapeDtypeStruct((2 * 64 * 64, 128), F32),
        ),
        in_specs=[vmem] * 4,
        out_specs=(hbm, vmem),
        scratch_shapes=[
            pltpu.VMEM((2, 2, 256, 128), F32),
            pltpu.VMEM((2, 256, 2 * BLOCK), F32),
            pltpu.SemaphoreType.DMA,
        ],
        input_output_aliases={0: 1},
        compiler_params=pltpu.CompilerParams(vmem_limit_bytes=40 << 20),
        name="refine",
    )(fine, odd, phase, stacked)
    return out.reshape(2, 8, 64, 8, 128).transpose(0, 1, 3, 2, 4).reshape(2, 64, 2 * OLD_N)


def solution(mesh):
    return jax.shard_map(
        on_device, mesh=mesh, in_specs=(P(None, "row", "col"),), out_specs=P(None, ("row", "col"), None), check_vma=False
    )
```
